128 devices in a mesh: ctx: 32 (over y, z, core), ch: 4 (over x).
Axes of the slice: x: 4, y: 4, z: 4, core: 2. Of those that a mesh axis runs over, the one named last changes fastest.
Arguments:
- branches: bfloat16 [16384, 3, 4096], P('ctx', None, 'ch'), may hold values from -6 to 6
- short_kernel: float32 [3, 3, 4096], P(None, None, 'ch'), may hold values from -3 to 3
- long_filter: float32 [16384, 4096], P('ctx', 'ch'), may hold values from -2 to 2
- skip_gain: float32 [4096], P('ch'), may hold values from -4 to 4
- out_weight: bfloat16 [4096, 4096], P('ch'), may hold values from -0.09375 to 0.09375
Outputs:
- mixed: bfloat16 [16384, 4096], P('ctx', 'ch')
The draws below stay inside these ranges and needn't reach their ends.
All inputs are finite; a program needn't handle non-finite values.
Results may differ from the reference program's by a relative error of at most 0.02.
Values may be sent and summed in bfloat16 or wider, within the bound.
A program may use at most 256 MiB of HBM per device.

```python
import jax
import jax.numpy as jnp

CH = 4096
KERNEL = 3
CONTEXT_SPAN = 16384


def draw_long_filter(key, part):
    key = jax.random.fold_in(key, 11)
    category_seed, quick_decay_seed, gradual_decay_seed, spike_random_seed, jitter_seed, floor_seed, floor_sign_seed, floor_rough_seed = jax.random.split(key, 8)
    slow_share = 5
    chooser = jax.random.randint(category_seed, (CH,), 0, 10)
    fast_tau = jnp.exp(jax.random.uniform(quick_decay_seed, (CH,), jnp.float32, jnp.log(12.0), jnp.log(2.0 * CONTEXT_SPAN)))
    slow_tau = jnp.exp(jax.random.uniform(gradual_decay_seed, (CH,), jnp.float32, jnp.log(2.0 * CONTEXT_SPAN), jnp.log(8.0 * CONTEXT_SPAN)))
    tau = jnp.where(chooser < slow_share, slow_tau, fast_tau)
    spike_occurrences = jax.random.randint(spike_random_seed, (3,), 1, CONTEXT_SPAN)
    context_indices = jnp.arange(CONTEXT_SPAN, dtype=jnp.int32)
    agreement_holds = jnp.sum((context_indices[:, None] >= spike_occurrences[None, :]).astype(jnp.float32), axis=1)
    steps_float = context_indices.astype(jnp.float32)[:, None]
    envelope = jnp.exp(-steps_float / tau[None, :]) * (0.7 ** agreement_holds)[:, None]
    envelope = envelope * jnp.sqrt(2.0 / jnp.minimum(tau, 1.0 * CONTEXT_SPAN))[None, :]
    noise = jnp.clip(jax.random.normal(jitter_seed, (CONTEXT_SPAN, CH), jnp.float32), -4.0, 4.0)
    floor_share = jnp.exp(jax.random.uniform(floor_seed, (CH,), jnp.float32, jnp.log(0.0003), jnp.log(0.002)))
    floor_sign = 2.0 * jax.random.randint(floor_sign_seed, (CH,), 0, 2).astype(jnp.float32) - 1.0
    floor_level = floor_sign * jnp.sqrt(floor_share / (1.0 * CONTEXT_SPAN))
    floor_rough = 0.6 + 0.8 * jax.random.uniform(floor_rough_seed, (CONTEXT_SPAN, CH), jnp.float32)
    return (noise * envelope + floor_level[None, :] * floor_rough).astype(jnp.float32)


def draw_branches(key, part):
    key = jax.random.fold_in(key, 5)
    noise_seed, sign_seed, level_seed = jax.random.split(key, 3)
    noise = jnp.clip(jax.random.normal(noise_seed, (CONTEXT_SPAN, 3, CH), jnp.float32), -4.0, 4.0)
    level = jax.random.uniform(level_seed, (2, CH), jnp.float32, 0.6, 1.2)
    signs = 2.0 * jax.random.randint(sign_seed, (2, CH), 0, 2).astype(jnp.float32) - 1.0
    means = jnp.concatenate([jnp.zeros((1, CH), jnp.float32), signs * level], axis=0)
    return (noise + means[None, :, :]).astype(jnp.bfloat16)


def level_of(rng, shape, cuts, least, largest):
    factor_of = 1.0
    for position, parts in cuts:
        steps = jax.random.uniform(jax.random.fold_in(jax.random.fold_in(rng, 6), position), (parts,), jnp.float32, least / len(cuts), largest / len(cuts))
        factor_of = factor_of * jnp.repeat(jnp.exp(steps), shape[position] // parts).reshape((-1,) + (1,) * (len(shape) - 1 - position))
    return factor_of


def centred(stream_key, extent, deviation, bound, pieces=(), kind=jnp.bfloat16):
    array = deviation * jax.random.normal(stream_key, extent, jnp.float32)
    if pieces:
        array = array * level_of(stream_key, extent, pieces, -0.22, 0.18)
    return jnp.clip(array, -bound, bound).astype(kind)


def setup_inputs(seed: int = 0) -> dict:
    seeds = jax.random.split(jax.random.key(seed), 6)
    return {
        "branches": draw_branches(jax.random.fold_in(seeds[5], 71), 0),
        "short_kernel": centred(seeds[1], (KERNEL, 3, CH), 0.6, 3.0, ((2, 4),), jnp.float32),
        "long_filter": draw_long_filter(jax.random.fold_in(seeds[5], 71), 0),
        "skip_gain": centred(seeds[3], (CH,), 1.0, 4.0, ((0, 4),), jnp.float32),
        "out_weight": centred(seeds[4], (CH, CH), CH ** -0.5, 0.09375, ((0, 4),)),
    }


def reference(branches, short_kernel, long_filter, skip_gain, out_weight):
    taps = short_kernel.shape[0]
    widened = branches.astype(jnp.float32)
    padded = jnp.pad(widened, ((taps - 1, 0), (0, 0), (0, 0)))
    featured = jnp.zeros_like(widened)
    for offset in range(taps):
        featured = featured + short_kernel[offset][None, :, :] * padded[taps - 1 - offset:taps - 1 - offset + CONTEXT_SPAN]
    query = featured[:, 0]
    driven = featured[:, 1] * featured[:, 2]
    driven_freq = jnp.fft.rfft(driven, n=2 * CONTEXT_SPAN, axis=0)
    filter_freq = jnp.fft.rfft(long_filter, n=2 * CONTEXT_SPAN, axis=0)
    long_conv = jnp.fft.irfft(driven_freq * filter_freq, n=2 * CONTEXT_SPAN, axis=0)[:CONTEXT_SPAN]
    long_conv = long_conv.astype(widened.dtype)
    gated = (query * (long_conv + skip_gain * driven)).astype(jnp.bfloat16)
    return jnp.dot(gated, out_weight, preferred_element_type=jnp.float32).astype(jnp.bfloat16)
```

```python
import functools
import math

import jax
import jax.numpy as jnp
import ml_dtypes
import numpy as np
from jax import lax
from jax.experimental import pallas as pl
from jax.experimental.pallas import tpu as pltpu
from jax.sharding import PartitionSpec as P

GROUP = 16


def tables(blocks, rows):
    classes = 2 * blocks
    half = blocks + 1
    length = classes * rows
    ids, places, blk = np.arange(half), np.arange(rows), np.arange(blocks)
    col = 2.0 * np.pi / classes * (np.outer(ids, blk) % classes)
    eye = np.eye(GROUP)
    first = np.concatenate([np.cos(col), -np.sin(col)[1:blocks]])
    weight = np.full((half, 1), 2.0)
    weight[0] = weight[blocks] = 1.0
    last = np.concatenate([weight * np.cos(col), (-weight * np.sin(col))[1:blocks]]).T / length
    twist = 2.0 * np.pi / length * (np.outer(ids, places) % length)
    inner = 2.0 * np.pi / rows * (np.outer(places, places) % rows)
    cos, sin = np.cos(inner), np.sin(inner)
    square = np.block([[cos, -sin], [sin, cos]])
    return (
        np.kron(first, eye).astype(ml_dtypes.bfloat16),
        np.kron(last, eye).astype(ml_dtypes.bfloat16),
        square.astype(ml_dtypes.bfloat16),
        np.cos(twist).astype(np.float32)[:, None, :],
        np.sin(twist).astype(np.float32)[:, None, :],
    )


def mul(left, right):
    return jnp.dot(left, right, preferred_element_type=jnp.float32)


def conv_kernel(blocks, rows, d_ref, h_ref, first, last, square, tw_cos, tw_sin, out_ref, col, turned, spec_d, spec_h, wide):
    half = blocks + 1
    chans = d_ref.shape[1]

    def forward(src, g, spec):
        x = src[:, pl.ds(g * GROUP, GROUP), :].reshape(blocks * GROUP, rows)
        col[...] = mul(first[...], x).reshape(2 * blocks, GROUP, rows)
        for k in range(half):
            c, s = tw_cos[k], tw_sin[k]
            re = col[k]
            if 0 < k < blocks:
                im = col[blocks + k]
                a, b = re * c + im * s, im * c - re * s
            else:
                a, b = re * c, -(re * s)
            turned[k, :, :rows] = a.astype(jnp.bfloat16)
            turned[k, :, rows:] = b.astype(jnp.bfloat16)
        spec[...] = mul(turned[...].reshape(half * GROUP, 2 * rows), square[...])

    def group(g, carry):
        forward(h_ref, g, spec_h)
        forward(d_ref, g, spec_d)
        a, b = spec_d[:, :rows], spec_d[:, rows:]
        u, v = spec_h[:, :rows], spec_h[:, rows:]
        flat = turned.reshape(half * GROUP, 2 * rows)
        flat[:, :rows] = (a * v + b * u).astype(jnp.bfloat16)
        flat[:, rows:] = (a * u - b * v).astype(jnp.bfloat16)
        spec_d[...] = mul(flat[...], square[...])
        back = spec_d.reshape(half, GROUP, 2 * rows)
        for k in range(half):
            c, s = tw_cos[k], tw_sin[k]
            im, re = back[k, :, :rows], back[k, :, rows:]
            wide[k] = (re * c - im * s).astype(jnp.bfloat16)
            if 0 < k < blocks:
                wide[blocks + k] = (im * c + re * s).astype(jnp.bfloat16)
        y = mul(last[...], wide[...].reshape(2 * blocks * GROUP, rows))
        out_ref[:, pl.ds(g * GROUP, GROUP), :] = y.reshape(blocks, GROUP, rows).astype(out_ref.dtype)
        return carry

    lax.fori_loop(0, chans // GROUP, group, 0)


def long_convolution(d, h):
    blocks, chans, rows = d.shape
    half = blocks + 1
    return pl.pallas_call(
        functools.partial(conv_kernel, blocks, rows),
        out_shape=jax.ShapeDtypeStruct(d.shape, jnp.bfloat16),
        in_specs=[pl.BlockSpec(memory_space=pltpu.VMEM)] * 7,
        out_specs=pl.BlockSpec(memory_space=pltpu.VMEM),
        scratch_shapes=[
            pltpu.VMEM((2 * blocks, GROUP, rows), jnp.float32),
            pltpu.VMEM((half, GROUP, 2 * rows), jnp.bfloat16),
            pltpu.VMEM((half * GROUP, 2 * rows), jnp.float32),
            pltpu.VMEM((half * GROUP, 2 * rows), jnp.float32),
            pltpu.VMEM((2 * blocks, GROUP, rows), jnp.bfloat16),
        ],
        compiler_params=pltpu.CompilerParams(vmem_limit_bytes=48 * 2**20),
        name="long_convolution",
    )(d, h, *tables(blocks, rows))


def passed_along(array, axis, by):
    count = lax.axis_size(axis)
    pairs = [(i, i + by) for i in range(count) if 0 <= i + by < count]
    return lax.ppermute(array, axis, pairs)


def on_device(branches, short_kernel, long_filter, skip_gain, out_weight):
    count = lax.axis_size("ctx")
    rows, _, chans = branches.shape
    taps = short_kernel.shape[0]

    def to_channels(x):
        x = x.astype(jnp.bfloat16).T.reshape(count, chans // count, rows)
        return lax.all_to_all(x, "ctx", split_axis=0, concat_axis=0, tiled=True)

    h = to_channels(long_filter)
    earlier = passed_along(branches[rows - (taps - 1):], "ctx", 1)
    extended = jnp.concatenate([earlier, branches], axis=0).astype(jnp.float32)
    featured = sum(
        short_kernel[j][None] * extended[taps - 1 - j:taps - 1 - j + rows] for j in range(taps)
    )
    query = featured[:, 0]
    driven = featured[:, 1] * featured[:, 2]
    d = to_channels(driven)
    y = long_convolution(d, h)
    y = lax.all_to_all(y, "ctx", split_axis=0, concat_axis=0, tiled=True)
    conv = y.reshape(chans, rows).T.astype(jnp.float32)
    gated = (query * (conv + skip_gain * driven)).astype(jnp.bfloat16)
    terms = jnp.dot(gated, out_weight, preferred_element_type=jnp.float32)
    return lax.psum_scatter(terms.astype(jnp.bfloat16), "ch", scatter_dimension=1, tiled=True)


def solution(mesh):
    placed = (P("ctx", None, "ch"), P(None, None, "ch"), P("ctx", "ch"), P("ch"), P("ch", None))
    return jax.shard_map(
        on_device, mesh=mesh, in_specs=placed, out_specs=P("ctx", "ch"), check_vma=False
    )
```

```python
import functools

import jax
import jax.numpy as jnp
import ml_dtypes
import numpy as np
from jax import lax
from jax.experimental import pallas as pl
from jax.experimental.pallas import tpu as pltpu
from jax.sharding import PartitionSpec as P

MESH = pl.DeviceIdType.MESH
GROUP = 16
TILE = 128


def tables(blocks, rows):
    classes = 2 * blocks
    half = blocks + 1
    length = classes * rows
    ids, places, blk = np.arange(half), np.arange(rows), np.arange(blocks)
    col = 2.0 * np.pi / classes * (np.outer(ids, blk) % classes)
    eye = np.eye(GROUP)
    first = np.concatenate([np.cos(col), -np.sin(col)[1:blocks]])
    weight = np.full((half, 1), 2.0)
    weight[0] = weight[blocks] = 1.0
    last = np.concatenate([weight * np.cos(col), (-weight * np.sin(col))[1:blocks]]).T / length
    twist = 2.0 * np.pi / length * (np.outer(ids, places) % length)
    inner = 2.0 * np.pi / rows * (np.outer(places, places) % rows)
    cos, sin = np.cos(inner), np.sin(inner)
    square = np.block([[cos, -sin], [sin, cos]])
    return (
        np.kron(first, eye).astype(ml_dtypes.bfloat16),
        np.kron(last, eye).astype(ml_dtypes.bfloat16),
        square.astype(ml_dtypes.bfloat16),
        np.cos(twist).astype(np.float32)[:, None, :],
        np.sin(twist).astype(np.float32)[:, None, :],
    )


def mul(left, right):
    return jnp.dot(left, right, preferred_element_type=jnp.float32)


def loop(count, body, start=0):
    def step(i, carry):
        body(i)
        return carry

    lax.fori_loop(start, count, step, 0)


def kernel(
    blocks, ring,
    br_in, taps_ref, filt_in, skip_ref, w_in, first_in, last_in, square_in, cos_in, sin_in,
    out_ref,
    br, filt, w, first, last, square, tw_cos, tw_sin,
    halo, h_send, d_send, h_recv, d_recv, y_send, y_recv,
    query, direct, gated, own,
    col, turned, spec_d, spec_h, wide,
    s1, r1, s2, r2,
    in_sem, halo_sem, h_sem, d_sem, y_sem, r1_sem, r2_sem, send_sem,
):
    me = lax.axis_index("ctx")
    x = lax.axis_index("ch")
    _, rows, chans = br.shape
    share = chans // blocks
    groups = share // GROUP
    half = blocks + 1
    quarters = rows // TILE
    right, left = lax.rem(x + 1, ring), lax.rem(x + ring - 1, ring)

    inputs = [
        pltpu.make_async_copy(src, dst, in_sem.at[i])
        for i, (src, dst) in enumerate([
            (filt_in, filt), (br_in, br), (first_in, first), (cos_in, tw_cos), (sin_in, tw_sin),
            (square_in, square), (last_in, last), (w_in, w),
        ])
    ]
    for copy in inputs:
        copy.start()

    barrier = pltpu.get_barrier_semaphore()

    def greet(k):
        pl.semaphore_signal(
            barrier, inc=1, device_id={"ctx": lax.rem(me + k, blocks)}, device_id_type=MESH
        )

    loop(blocks, greet, 1)
    for side in (left, right):
        pl.semaphore_signal(barrier, inc=1, device_id={"ch": side}, device_id_type=MESH)

    def lanes(i):
        return pl.ds(pl.multiple_of(i * TILE, TILE), TILE)

    def turn_filter(i):
        for r in range(quarters):
            here = slice(r * TILE, (r + 1) * TILE)
            h_send[lanes(i), here] = filt[here, lanes(i)].T.astype(jnp.bfloat16)

    def feature(r, i):
        here = slice(r * TILE, (r + 1) * TILE)
        feats = []
        for b in range(3):
            if r:
                part = br[b, r * TILE - GROUP:(r + 1) * TILE, lanes(i)].astype(jnp.float32)
            else:
                before = halo[b, :, lanes(i)].astype(jnp.float32)
                before = jnp.where(me > 0, before, jnp.zeros_like(before))
                part = jnp.concatenate([before, br[b, here, lanes(i)].astype(jnp.float32)], axis=0)
            total = taps_ref[0, b:b + 1, lanes(i)] * part[GROUP:]
            for j in (1, 2):
                total = total + taps_ref[j, b:b + 1, lanes(i)] * pltpu.roll(part, j, 0)[GROUP:]
            feats.append(total)
        driven = feats[1] * feats[2]
        query[here, lanes(i)] = feats[0]
        direct[here, lanes(i)] = skip_ref[:, lanes(i)] * driven
        d_send[lanes(i), here] = driven.T.astype(jnp.bfloat16)

    inputs[0].wait()
    loop(chans // TILE, turn_filter)
    inputs[1].wait()
    for r in range(1, quarters):
        loop(chans // TILE, functools.partial(feature, r))

    pl.semaphore_wait(barrier, blocks - 1 + 2)

    halo_copy = pltpu.make_async_remote_copy(
        src_ref=br.at[:, pl.ds(rows - GROUP, GROUP), :],
        dst_ref=halo,
        send_sem=send_sem.at[0],
        recv_sem=halo_sem.at[0],
        device_id={"ctx": lax.rem(me + 1, blocks)},
        device_id_type=MESH,
    )
    halo_copy.start()

    def scatter(src, dst, send, recv):
        def one(k):
            t = lax.rem(me + k, blocks)
            pltpu.make_async_remote_copy(
                src_ref=src(t), dst_ref=dst, send_sem=send, recv_sem=recv,
                device_id={"ctx": t}, device_id_type=MESH,
            ).start()

        loop(blocks, one, 1)
        pltpu.make_async_copy(src(me), dst, recv).start()

    def block(t):
        return pl.ds(pl.multiple_of(t * share, share), share)

    def part_of(t, g):
        return pl.ds(pl.multiple_of(t * share + g * GROUP, GROUP), GROUP)

    scatter(lambda t: h_send.at[block(t)], h_recv.at[me], send_sem.at[1], h_sem.at[0])
    halo_copy.wait_recv()
    loop(chans // TILE, functools.partial(feature, 0))
    for g in range(groups):
        scatter(lambda t: d_send.at[part_of(t, g)], d_recv.at[g, me], send_sem.at[2], d_sem.at[g])

    def arrived(ref, sem):
        pltpu.make_async_copy(ref, ref, sem).wait()

    def forward(blocks_in, spec):
        col[...] = mul(first[...], blocks_in.reshape(blocks * GROUP, rows)).reshape(2 * blocks, GROUP, rows)
        for k in range(half):
            c, s = tw_cos[k], tw_sin[k]
            re = col[k]
            if 0 < k < blocks:
                im = col[blocks + k]
                a, b = re * c + im * s, im * c - re * s
            else:
                a, b = re * c, -(re * s)
            turned[k, :, :rows] = a.astype(jnp.bfloat16)
            turned[k, :, rows:] = b.astype(jnp.bfloat16)
        spec[...] = mul(turned[...].reshape(half * GROUP, 2 * rows), square[...])

    for copy in inputs[2:7]:
        copy.wait()
    arrived(h_recv, h_sem.at[0])

    def filter_group(g):
        forward(h_recv[:, pl.ds(pl.multiple_of(g * GROUP, GROUP), GROUP), :], spec_h.at[g])

    loop(groups, filter_group)

    def driven_group(g):
        arrived(d_recv.at[g], d_sem.at[g])
        forward(d_recv[g], spec_d)
        a, b = spec_d[:, :rows], spec_d[:, rows:]
        u, v = spec_h[g, :, :rows], spec_h[g, :, rows:]
        flat = turned.reshape(half * GROUP, 2 * rows)
        flat[:, :rows] = (a * v + b * u).astype(jnp.bfloat16)
        flat[:, rows:] = (a * u - b * v).astype(jnp.bfloat16)
        spec_d[...] = mul(flat[...], square[...])
        back = spec_d.reshape(half, GROUP, 2 * rows)
        for k in range(half):
            c, s = tw_cos[k], tw_sin[k]
            im, re = back[k, :, :rows], back[k, :, rows:]
            wide[k] = (re * c - im * s).astype(jnp.bfloat16)
            if 0 < k < blocks:
                wide[blocks + k] = (im * c + re * s).astype(jnp.bfloat16)
        y = mul(last[...], wide[...].reshape(2 * blocks * GROUP, rows)).astype(jnp.bfloat16)
        for q in range(quarters):
            y_send[q, :, pl.ds(pl.multiple_of(g * GROUP, GROUP), GROUP), :] = y[
                :, q * TILE:(q + 1) * TILE
            ].reshape(blocks, GROUP, TILE)

    loop(groups, driven_group)

    def give_back(q):
        scatter(lambda t: y_send.at[q, t], y_recv.at[q, me], send_sem.at[3], y_sem.at[q])

    loop(quarters, give_back)
    inputs[7].wait()

    def quarter(q):
        return pl.ds(pl.multiple_of(q * TILE, TILE), TILE)

    def project(q, target):
        columns = pl.ds(pl.multiple_of(target * chans, chans), chans)
        return mul(gated[quarter(q)], w[:, columns])

    def push(src, dst, send, recv, side):
        pltpu.make_async_remote_copy(
            src_ref=src, dst_ref=dst, send_sem=send, recv_sem=recv,
            device_id={"ch": side}, device_id_type=MESH,
        ).start()

    def opposite(q):
        arrived(y_recv.at[q], y_sem.at[q])

        def gate(i):
            per = TILE // share
            turned_back = y_recv[q, pl.ds(i * per, per)].reshape(TILE, TILE).astype(jnp.float32).T
            value = query[quarter(q), lanes(i)] * (turned_back + direct[quarter(q), lanes(i)])
            gated[quarter(q), lanes(i)] = value.astype(jnp.bfloat16)

        loop(chans // TILE, gate)
        terms = project(q, lax.rem(x + 2, ring)).astype(jnp.bfloat16)
        s1[0, q] = terms[:TILE // 2]
        s1[1, q] = terms[TILE // 2:]
        push(s1.at[0, q], r1.at[0, q], send_sem.at[4], r1_sem.at[0, q], right)
        push(s1.at[1, q], r1.at[1, q], send_sem.at[4], r1_sem.at[1, q], left)

    def beside(q):
        for side, (target, lo, hi) in enumerate([(right, 0, TILE // 2), (left, TILE // 2, TILE)]):
            terms = project(q, target)
            arrived(r1.at[side, q], r1_sem.at[side, q])
            s2[side, q, lo:hi] = (terms[lo:hi] + r1[side, q].astype(jnp.float32)).astype(jnp.bfloat16)
            other = slice(TILE // 2 - lo, TILE + TILE // 2 - hi)
            s2[side, q, other] = terms[other].astype(jnp.bfloat16)
            push(s2.at[side, q], r2.at[side, q], send_sem.at[5], r2_sem.at[side, q], target)
        own[quarter(q)] = project(q, x)

    opposite(0)

    def steady(q):
        opposite(q + 1)
        beside(q)

    loop(quarters - 1, steady)
    beside(quarters - 1)

    def finish(q):
        for side in range(2):
            arrived(r2.at[side, q], r2_sem.at[side, q])
        total = own[quarter(q)] + r2[0, q].astype(jnp.float32) + r2[1, q].astype(jnp.float32)
        out_ref[quarter(q)] = total.astype(out_ref.dtype)

    loop(quarters, finish)

    halo_copy.wait_send()
    arrived(h_send.at[pl.ds(0, chans - share)], send_sem.at[1])
    arrived(d_send.at[pl.ds(0, chans - share)], send_sem.at[2])
    others = y_send.at[:, pl.ds(0, blocks - 1)]
    arrived(others, send_sem.at[3])
    arrived(s1, send_sem.at[4])
    arrived(s2, send_sem.at[5])


def on_device(branches, short_kernel, long_filter, skip_gain, out_weight):
    blocks, ring = lax.axis_size("ctx"), lax.axis_size("ch")
    rows, _, chans = branches.shape
    share, half, quarters = chans // blocks, blocks + 1, rows // TILE
    groups = share // GROUP
    bf16, f32 = jnp.bfloat16, jnp.float32
    consts = tables(blocks, rows)
    anywhere, vmem = pl.BlockSpec(memory_space=pl.ANY), pl.BlockSpec(memory_space=pltpu.VMEM)
    dma = pltpu.SemaphoreType.DMA
    scratch = [
        pltpu.VMEM((3, rows, chans), bf16),
        pltpu.VMEM((rows, chans), f32),
        pltpu.VMEM(out_weight.shape, bf16),
        *[pltpu.VMEM(t.shape, t.dtype) for t in consts],
        pltpu.VMEM((3, GROUP, chans), bf16),
        pltpu.VMEM((chans, rows), bf16),
        pltpu.VMEM((chans, rows), bf16),
        pltpu.VMEM((blocks, share, rows), bf16),
        pltpu.VMEM((groups, blocks, GROUP, rows), bf16),
        pltpu.VMEM((quarters, blocks, share, TILE), bf16),
        pltpu.VMEM((quarters, blocks, share, TILE), bf16),
        pltpu.VMEM((rows, chans), f32),
        pltpu.VMEM((rows, chans), f32),
        pltpu.VMEM((rows, chans), bf16),
        pltpu.VMEM((rows, chans), f32),
        pltpu.VMEM((2 * blocks, GROUP, rows), f32),
        pltpu.VMEM((half, GROUP, 2 * rows), bf16),
        pltpu.VMEM((half * GROUP, 2 * rows), f32),
        pltpu.VMEM((groups, half * GROUP, 2 * rows), f32),
        pltpu.VMEM((2 * blocks, GROUP, rows), bf16),
        pltpu.VMEM((2, quarters, TILE // 2, chans), bf16),
        pltpu.VMEM((2, quarters, TILE // 2, chans), bf16),
        pltpu.VMEM((2, quarters, TILE, chans), bf16),
        pltpu.VMEM((2, quarters, TILE, chans), bf16),
        dma((8,)), dma((1,)), dma((1,)), dma((groups,)), dma((quarters,)),
        dma((2, quarters)), dma((2, quarters)), dma((6,)),
    ]
    return pl.pallas_call(
        functools.partial(kernel, blocks, ring),
        out_shape=jax.ShapeDtypeStruct((rows, chans), bf16),
        in_specs=[anywhere, vmem, anywhere, vmem] + [anywhere] * 6,
        out_specs=vmem,
        scratch_shapes=scratch,
        compiler_params=pltpu.CompilerParams(
            collective_id=0, has_side_effects=True, vmem_limit_bytes=60 * 2**20
        ),
        name="hyena_operator",
    )(
        jnp.transpose(branches, (1, 0, 2)), short_kernel, long_filter, skip_gain.reshape(1, chans),
        out_weight, *consts,
    )


def solution(mesh):
    placed = (P("ctx", None, "ch"), P(None, None, "ch"), P("ctx", "ch"), P("ch"), P("ch", None))
    return jax.shard_map(
        on_device, mesh=mesh, in_specs=placed, out_specs=P("ctx", "ch"), check_vma=False
    )
```

```python
import functools

import jax
import jax.numpy as jnp
import ml_dtypes
import numpy as np
from jax import lax
from jax.experimental import pallas as pl
from jax.experimental.pallas import tpu as pltpu
from jax.sharding import PartitionSpec as P

MESH = pl.DeviceIdType.MESH
GROUP = 16
TILE = 128


def tables(blocks, rows):
    classes = 2 * blocks
    half = blocks + 1
    length = classes * rows
    ids, places, blk = np.arange(half), np.arange(rows), np.arange(blocks)
    col = 2.0 * np.pi / classes * (np.outer(ids, blk) % classes)
    eye = np.eye(GROUP)
    first = np.concatenate([np.cos(col), -np.sin(col)[1:blocks]])
    weight = np.full((half, 1), 2.0)
    weight[0] = weight[blocks] = 1.0
    last = np.concatenate([weight * np.cos(col), (-weight * np.sin(col))[1:blocks]]).T / length
    twist = 2.0 * np.pi / length * (np.outer(ids, places) % length)
    inner = 2.0 * np.pi / rows * (np.outer(places, places) % rows)
    cos, sin = np.cos(inner), np.sin(inner)
    square = np.block([[cos, -sin], [sin, cos]])
    return (
        np.kron(first, eye).astype(ml_dtypes.bfloat16),
        np.kron(last, eye).astype(ml_dtypes.bfloat16),
        square.astype(ml_dtypes.bfloat16),
        np.cos(twist).astype(np.float32)[:, None, :],
        np.sin(twist).astype(np.float32)[:, None, :],
    )


def mul(left, right):
    return jnp.dot(left, right, preferred_element_type=jnp.float32)


def loop(count, body, start=0):
    def step(i, carry):
        body(i)
        return carry

    lax.fori_loop(start, count, step, 0)


def kernel(
    blocks, ring,
    br_in, taps_ref, filt_in, skip_ref, w_in, first_in, last_in, square_in, cos_in, sin_in,
    out_ref,
    br, filt, w, first, last, square, tw_cos, tw_sin,
    halo, h_send, d_send, h_recv, d_recv, y_send, y_recv,
    query, direct, gated, own,
    col, turned, spec_d, spec_h, wide,
    s1, r1, s2, r2,
    in_sem, halo_sem, h_sem, d_sem, y_sem, r1_sem, r2_sem, send_sem,
):
    me = lax.axis_index("ctx")
    x = lax.axis_index("ch")
    _, rows, chans = br.shape
    groups = chans // blocks // GROUP
    per = TILE // GROUP
    owners = blocks // per
    half = blocks + 1
    quarters = rows // TILE
    right, left = lax.rem(x + 1, ring), lax.rem(x + ring - 1, ring)

    inputs = [
        pltpu.make_async_copy(src, dst, in_sem.at[i])
        for i, (src, dst) in enumerate([
            (filt_in, filt), (br_in, br), (first_in, first), (cos_in, tw_cos), (sin_in, tw_sin),
            (square_in, square), (last_in, last), (w_in, w),
        ])
    ]
    for copy in inputs[:2]:
        copy.start()

    barrier = pltpu.get_barrier_semaphore()

    def greet(k):
        pl.semaphore_signal(
            barrier, inc=1, device_id={"ctx": lax.rem(me + k, blocks)}, device_id_type=MESH
        )

    loop(blocks, greet, 1)
    for side in (left, right):
        pl.semaphore_signal(barrier, inc=1, device_id={"ch": side}, device_id_type=MESH)

    def lanes(i):
        return pl.ds(pl.multiple_of(i * TILE, TILE), TILE)

    def feature(r, i):
        here = slice(r * TILE, (r + 1) * TILE)
        feats = []
        for b in range(3):
            if r:
                part = br[b, r * TILE - GROUP:(r + 1) * TILE, lanes(i)].astype(jnp.float32)
            else:
                before = halo[b, :, lanes(i)].astype(jnp.float32)
                before = jnp.where(me > 0, before, jnp.zeros_like(before))
                part = jnp.concatenate([before, br[b, here, lanes(i)].astype(jnp.float32)], axis=0)
            total = taps_ref[0, b:b + 1, lanes(i)] * part[GROUP:]
            for j in (1, 2):
                total = total + taps_ref[j, b:b + 1, lanes(i)] * pltpu.roll(part, j, 0)[GROUP:]
            feats.append(total)
        driven = feats[1] * feats[2]
        query[here, lanes(i)] = feats[0]
        direct[here, lanes(i)] = skip_ref[:, lanes(i)] * driven
        g, t = i // owners, lax.rem(i, owners) * per
        d_send[g, pl.ds(t, per), :, here] = driven.T.astype(jnp.bfloat16).reshape(per, GROUP, TILE)

    def ctx_copy(src, dst, send, recv, t):
        return pltpu.make_async_remote_copy(
            src_ref=src, dst_ref=dst, send_sem=send, recv_sem=recv,
            device_id={"ctx": t}, device_id_type=MESH,
        )

    def scatter(src, dst, send, recv):
        def one(k):
            t = lax.rem(me + k, blocks)
            ctx_copy(src(t), dst, send, recv, t).start()

        loop(blocks, one, 1)
        pltpu.make_async_copy(src(me), dst, recv).start()

    def arrived(ref, sem):
        pltpu.make_async_copy(ref, ref, sem).wait()

    halo_copy = ctx_copy(
        br_in.at[:, pl.ds(rows - GROUP, GROUP), :], halo, send_sem.at[0], halo_sem.at[0],
        lax.rem(me + 1, blocks),
    )

    def turn_filter(k):
        g, t = k // owners, lax.rem(me // per + k, owners)
        i = g * owners + t
        for r in range(quarters):
            here = slice(r * TILE, (r + 1) * TILE)
            turned_part = filt[here, lanes(i)].T.astype(jnp.bfloat16)
            h_send[g, pl.ds(t * per, per), :, here] = turned_part.reshape(per, GROUP, TILE)

        def one(j):
            to = t * per + lax.rem(me + j, per)
            src, dst = h_send.at[g, to], h_recv.at[g, me]

            @pl.when(to == me)
            def _():
                pltpu.make_async_copy(src, dst, h_sem.at[g]).start()

            @pl.when(to != me)
            def _():
                ctx_copy(src, dst, send_sem.at[1], h_sem.at[g], to).start()

        loop(per, one)

    inputs[0].wait()
    pl.semaphore_wait(barrier, blocks - 1 + 2)
    halo_copy.start()
    loop(chans // TILE, turn_filter)
    for copy in inputs[2:]:
        copy.start()
    inputs[1].wait()
    for r in range(1, quarters):
        loop(chans // TILE, functools.partial(feature, r))
    halo_copy.wait_recv()
    loop(chans // TILE, functools.partial(feature, 0))
    for g in range(groups):
        scatter(lambda t: d_send.at[g, t], d_recv.at[g, me], send_sem.at[2], d_sem.at[g])

    def forward(blocks_in, spec):
        col[...] = mul(first[...], blocks_in.reshape(blocks * GROUP, rows)).reshape(2 * blocks, GROUP, rows)
        for k in range(half):
            c, s = tw_cos[k], tw_sin[k]
            re = col[k]
            if 0 < k < blocks:
                im = col[blocks + k]
                a, b = re * c + im * s, im * c - re * s
            else:
                a, b = re * c, -(re * s)
            turned[k, :, :rows] = a.astype(jnp.bfloat16)
            turned[k, :, rows:] = b.astype(jnp.bfloat16)
        spec[...] = mul(turned[...].reshape(half * GROUP, 2 * rows), square[...])

    for copy in inputs[2:7]:
        copy.wait()

    def filter_group(g):
        arrived(h_recv.at[g], h_sem.at[g])
        forward(h_recv[g], spec_h.at[g])

    loop(groups, filter_group)

    def driven_group(g):
        arrived(d_recv.at[g], d_sem.at[g])
        forward(d_recv[g], spec_d)
        a, b = spec_d[:, :rows], spec_d[:, rows:]
        u, v = spec_h[g, :, :rows], spec_h[g, :, rows:]
        flat = turned.reshape(half * GROUP, 2 * rows)
        flat[:, :rows] = (a * v + b * u).astype(jnp.bfloat16)
        flat[:, rows:] = (a * u - b * v).astype(jnp.bfloat16)
        spec_d[...] = mul(flat[...], square[...])
        back = spec_d.reshape(half, GROUP, 2 * rows)
        for k in range(half):
            c, s = tw_cos[k], tw_sin[k]
            im, re = back[k, :, :rows], back[k, :, rows:]
            wide[k] = (re * c - im * s).astype(jnp.bfloat16)
            if 0 < k < blocks:
                wide[blocks + k] = (im * c + re * s).astype(jnp.bfloat16)
        for p in range(0, quarters, 2):
            y = mul(last[...], wide[:, :, p * TILE:(p + 2) * TILE].reshape(2 * blocks * GROUP, 2 * TILE))
            for q in (p, p + 1):
                part = y[:, (q - p) * TILE:(q - p + 1) * TILE].astype(jnp.bfloat16)
                y_send[q, g] = part.reshape(blocks, GROUP, TILE)
                scatter(
                    lambda t: y_send.at[q, g, t], y_recv.at[q, g, me], send_sem.at[3], y_sem.at[q, g]
                )

    loop(groups, driven_group)
    inputs[7].wait()

    def quarter(q):
        return pl.ds(pl.multiple_of(q * TILE, TILE), TILE)

    def project(q, target):
        columns = pl.ds(pl.multiple_of(target * chans, chans), chans)
        return mul(gated[quarter(q)], w[:, columns])

    def push(src, dst, send, recv, side):
        pltpu.make_async_remote_copy(
            src_ref=src, dst_ref=dst, send_sem=send, recv_sem=recv,
            device_id={"ch": side}, device_id_type=MESH,
        ).start()

    def opposite(q):
        for g in range(groups):
            arrived(y_recv.at[q, g], y_sem.at[q, g])

        def gate(i):
            g, t = i // owners, lax.rem(i, owners) * per
            turned_back = y_recv[q, g, pl.ds(t, per)].reshape(TILE, TILE).astype(jnp.float32).T
            value = query[quarter(q), lanes(i)] * (turned_back + direct[quarter(q), lanes(i)])
            gated[quarter(q), lanes(i)] = value.astype(jnp.bfloat16)

        loop(chans // TILE, gate)
        terms = project(q, lax.rem(x + 2, ring)).astype(jnp.bfloat16)
        s1[0, q] = terms[:TILE // 2]
        s1[1, q] = terms[TILE // 2:]
        push(s1.at[0, q], r1.at[0, q], send_sem.at[4], r1_sem.at[0, q], right)
        push(s1.at[1, q], r1.at[1, q], send_sem.at[4], r1_sem.at[1, q], left)

    def beside(q):
        for side, (target, lo, hi) in enumerate([(right, 0, TILE // 2), (left, TILE // 2, TILE)]):
            terms = project(q, target)
            arrived(r1.at[side, q], r1_sem.at[side, q])
            s2[side, q, lo:hi] = (terms[lo:hi] + r1[side, q].astype(jnp.float32)).astype(jnp.bfloat16)
            other = slice(TILE // 2 - lo, TILE + TILE // 2 - hi)
            s2[side, q, other] = terms[other].astype(jnp.bfloat16)
            push(s2.at[side, q], r2.at[side, q], send_sem.at[5], r2_sem.at[side, q], target)
        own[quarter(q)] = project(q, x)

    opposite(0)

    def steady(q):
        opposite(q + 1)
        beside(q)

    loop(quarters - 1, steady)
    beside(quarters - 1)

    def finish(q):
        for side in range(2):
            arrived(r2.at[side, q], r2_sem.at[side, q])
        total = own[quarter(q)] + r2[0, q].astype(jnp.float32) + r2[1, q].astype(jnp.float32)
        out_ref[quarter(q)] = total.astype(out_ref.dtype)

    loop(quarters, finish)

    halo_copy.wait_send()
    arrived(h_send.at[:, pl.ds(0, blocks - 1)], send_sem.at[1])
    arrived(d_send.at[:, pl.ds(0, blocks - 1)], send_sem.at[2])
    arrived(y_send.at[:, :, pl.ds(0, blocks - 1)], send_sem.at[3])
    arrived(s1, send_sem.at[4])
    arrived(s2, send_sem.at[5])


def on_device(branches, short_kernel, long_filter, skip_gain, out_weight):
    blocks, ring = lax.axis_size("ctx"), lax.axis_size("ch")
    rows, _, chans = branches.shape
    half, quarters, groups = blocks + 1, rows // TILE, chans // blocks // GROUP
    bf16, f32 = jnp.bfloat16, jnp.float32
    consts = tables(blocks, rows)
    anywhere, vmem = pl.BlockSpec(memory_space=pl.ANY), pl.BlockSpec(memory_space=pltpu.VMEM)
    dma = pltpu.SemaphoreType.DMA
    scratch = [
        pltpu.VMEM((3, rows, chans), bf16),
        pltpu.VMEM((rows, chans), f32),
        pltpu.VMEM(out_weight.shape, bf16),
        *[pltpu.VMEM(t.shape, t.dtype) for t in consts],
        pltpu.VMEM((3, GROUP, chans), bf16),
        *[pltpu.VMEM((groups, blocks, GROUP, rows), bf16)] * 4,
        *[pltpu.VMEM((quarters, groups, blocks, GROUP, TILE), bf16)] * 2,
        pltpu.VMEM((rows, chans), f32),
        pltpu.VMEM((rows, chans), f32),
        pltpu.VMEM((rows, chans), bf16),
        pltpu.VMEM((rows, chans), f32),
        pltpu.VMEM((2 * blocks, GROUP, rows), f32),
        pltpu.VMEM((half, GROUP, 2 * rows), bf16),
        pltpu.VMEM((half * GROUP, 2 * rows), f32),
        pltpu.VMEM((groups, half * GROUP, 2 * rows), f32),
        pltpu.VMEM((2 * blocks, GROUP, rows), bf16),
        pltpu.VMEM((2, quarters, TILE // 2, chans), bf16),
        pltpu.VMEM((2, quarters, TILE // 2, chans), bf16),
        pltpu.VMEM((2, quarters, TILE, chans), bf16),
        pltpu.VMEM((2, quarters, TILE, chans), bf16),
        dma((8,)), dma((1,)), dma((groups,)), dma((groups,)), dma((quarters, groups)),
        dma((2, quarters)), dma((2, quarters)), dma((6,)),
    ]
    return pl.pallas_call(
        functools.partial(kernel, blocks, ring),
        out_shape=pltpu.VMEM((rows, chans), bf16),
        in_specs=[anywhere, vmem, anywhere, vmem] + [anywhere] * 6,
        out_specs=vmem,
        scratch_shapes=scratch,
        compiler_params=pltpu.CompilerParams(
            collective_id=0, has_side_effects=True, vmem_limit_bytes=60 * 2**20
        ),
        name="hyena_operator",
    )(
        jnp.transpose(branches, (1, 0, 2)), short_kernel, long_filter, skip_gain.reshape(1, chans),
        out_weight, *consts,
    )


def solution(mesh):
    placed = (P("ctx", None, "ch"), P(None, None, "ch"), P("ctx", "ch"), P("ch"), P("ch", None))
    return jax.shard_map(
        on_device, mesh=mesh, in_specs=placed, out_specs=P("ctx", "ch"), check_vma=False
    )
```

```python
import functools

import jax
import jax.numpy as jnp
import ml_dtypes
import numpy as np
from jax import lax
from jax.experimental import pallas as pl
from jax.experimental.pallas import tpu as pltpu
from jax.sharding import PartitionSpec as P

MESH = pl.DeviceIdType.MESH
GROUP = 16
TILE = 128
AHEAD = 2
SHARED = 768


def tables(blocks, rows):
    classes = 2 * blocks
    half = blocks + 1
    length = classes * rows
    ids, places, blk = np.arange(half), np.arange(rows), np.arange(blocks)
    col = 2.0 * np.pi / classes * (np.outer(ids, blk) % classes)
    eye = np.eye(GROUP)
    first = np.concatenate([np.cos(col), -np.sin(col)[1:blocks]])
    weight = np.full((half, 1), 2.0)
    weight[0] = weight[blocks] = 1.0
    last = np.concatenate([weight * np.cos(col), (-weight * np.sin(col))[1:blocks]]).T / length
    twist = 2.0 * np.pi / length * (np.outer(ids, places) % length)
    inner = 2.0 * np.pi / rows * (np.outer(places, places) % rows)
    cos, sin = np.cos(inner), np.sin(inner)
    square = np.block([[cos, -sin], [sin, cos]])
    return (
        np.kron(first, eye).astype(ml_dtypes.bfloat16),
        np.kron(last, eye).astype(ml_dtypes.bfloat16),
        square.astype(ml_dtypes.bfloat16),
        np.cos(twist).astype(np.float32)[:, None, :],
        np.sin(twist).astype(np.float32)[:, None, :],
    )


def mul(left, right):
    return jnp.dot(left, right, preferred_element_type=jnp.float32)


def loop(count, body, start=0):
    def step(i, carry):
        body(i)
        return carry

    lax.fori_loop(start, count, step, 0)


def kernel(
    blocks, ring,
    br_in, taps_ref, filt_in, skip_ref, w_in, first_in, last_in, square_in, cos_in, sin_in,
    out_ref,
    br, filt, w, first, last, square, tw_cos, tw_sin,
    halo, h_send, d_send, h_recv, d_recv, y_send, y_recv,
    query, direct, gated, own,
    col, turned, spec_d, spec_h, wide,
    w_mate, gated_mate, pair_send, pair_recv, s1, r1, s2, r2,
    in_sem, halo_sem, h_sem, d_sem, y_sem, w_sem, g_sem, p_sem, r1_sem, r2_sem, send_sem,
):
    me = lax.axis_index("ctx")
    x = lax.axis_index("ch")
    _, rows, chans = br.shape
    groups = chans // blocks // GROUP
    per = TILE // GROUP
    owners = blocks // per
    half = blocks + 1
    quarters = rows // TILE
    right, left, across = lax.rem(x + 1, ring), lax.rem(x + ring - 1, ring), lax.rem(x + ring // 2, ring)
    swap = lax.rem(x, 2) * lax.rem(me + 1, 2) + lax.rem(x + 1, 2) * lax.rem(me, 2)
    mate, pair = right + swap * (left - right), left + swap * (right - left)

    inputs = [
        pltpu.make_async_copy(src, dst, in_sem.at[i])
        for i, (src, dst) in enumerate([
            (filt_in, filt), (br_in, br), (first_in, first), (cos_in, tw_cos), (sin_in, tw_sin),
            (square_in, square), (last_in, last), (w_in, w),
        ])
    ]
    for copy in inputs[:2]:
        copy.start()

    barrier = pltpu.get_barrier_semaphore()

    def greet(k):
        pl.semaphore_signal(
            barrier, inc=1, device_id={"ctx": lax.rem(me + k, blocks)}, device_id_type=MESH
        )

    loop(blocks, greet, 1)
    for side in (left, right):
        pl.semaphore_signal(barrier, inc=1, device_id={"ch": side}, device_id_type=MESH)

    def lanes(i):
        return pl.ds(pl.multiple_of(i * TILE, TILE), TILE)

    def feature(r, i):
        here = slice(r * TILE, (r + 1) * TILE)
        feats = []
        for b in range(3):
            if r:
                part = br[b, r * TILE - GROUP:(r + 1) * TILE, lanes(i)].astype(jnp.float32)
            else:
                before = halo[b, :, lanes(i)].astype(jnp.float32)
                before = jnp.where(me > 0, before, jnp.zeros_like(before))
                part = jnp.concatenate([before, br[b, here, lanes(i)].astype(jnp.float32)], axis=0)
            total = taps_ref[0, b:b + 1, lanes(i)] * part[GROUP:]
            for j in (1, 2):
                total = total + taps_ref[j, b:b + 1, lanes(i)] * pltpu.roll(part, j, 0)[GROUP:]
            feats.append(total)
        driven = feats[1] * feats[2]
        query[here, lanes(i)] = feats[0]
        direct[here, lanes(i)] = skip_ref[:, lanes(i)] * driven
        g, t = i // owners, lax.rem(i, owners) * per
        d_send[g, pl.ds(t, per), :, here] = driven.T.astype(jnp.bfloat16).reshape(per, GROUP, TILE)

    def ctx_copy(src, dst, send, recv, t):
        return pltpu.make_async_remote_copy(
            src_ref=src, dst_ref=dst, send_sem=send, recv_sem=recv,
            device_id={"ctx": t}, device_id_type=MESH,
        )

    def scatter(src, dst, send, recv):
        def one(k):
            t = lax.rem(me + k, blocks)
            ctx_copy(src(t), dst, send, recv, t).start()

        loop(blocks, one, 1)
        pltpu.make_async_copy(src(me), dst, recv).start()

    def push(src, dst, send, recv, side):
        pltpu.make_async_remote_copy(
            src_ref=src, dst_ref=dst, send_sem=send, recv_sem=recv,
            device_id={"ch": side}, device_id_type=MESH,
        ).start()

    def arrived(ref, sem):
        pltpu.make_async_copy(ref, ref, sem).wait()

    halo_copy = ctx_copy(
        br_in.at[:, pl.ds(rows - GROUP, GROUP), :], halo, send_sem.at[0], halo_sem.at[0],
        lax.rem(me + 1, blocks),
    )

    def turn_filter(k):
        g, t = k // owners, lax.rem(me // per + k, owners)
        i = g * owners + t
        for r in range(quarters):
            here = slice(r * TILE, (r + 1) * TILE)
            turned_part = filt[here, lanes(i)].T.astype(jnp.bfloat16)
            h_send[g, pl.ds(t * per, per), :, here] = turned_part.reshape(per, GROUP, TILE)

        def one(j):
            to = t * per + lax.rem(me + j, per)
            src, dst = h_send.at[g, to], h_recv.at[g, me]

            @pl.when(to == me)
            def _():
                pltpu.make_async_copy(src, dst, h_sem.at[g]).start()

            @pl.when(to != me)
            def _():
                ctx_copy(src, dst, send_sem.at[1], h_sem.at[g], to).start()

        loop(per, one)

    inputs[0].wait()
    pl.semaphore_wait(barrier, blocks - 1 + 2)
    for i, target in enumerate((mate, across)):
        push(
            w_in.at[:, pl.ds(pl.multiple_of(target * chans, chans), SHARED)], w_mate.at[i],
            send_sem.at[6], w_sem.at[i], mate,
        )
    halo_copy.start()
    loop(chans // TILE, turn_filter)
    for copy in inputs[2:]:
        copy.start()
    inputs[1].wait()
    for r in range(1, quarters):
        loop(chans // TILE, functools.partial(feature, r))
    halo_copy.wait_recv()
    loop(chans // TILE, functools.partial(feature, 0))
    def send_driven(g):
        scatter(lambda t: d_send.at[g, t], d_recv.at[g, me], send_sem.at[2], d_sem.at[g])

    arrived(h_send.at[:, pl.ds(0, blocks - 1)], send_sem.at[1])
    send_driven(0)

    def forward(blocks_in, spec):
        col[...] = mul(first[...], blocks_in.reshape(blocks * GROUP, rows)).reshape(2 * blocks, GROUP, rows)
        for k in range(half):
            c, s = tw_cos[k], tw_sin[k]
            re = col[k]
            if 0 < k < blocks:
                im = col[blocks + k]
                a, b = re * c + im * s, im * c - re * s
            else:
                a, b = re * c, -(re * s)
            turned[k, :, :rows] = a.astype(jnp.bfloat16)
            turned[k, :, rows:] = b.astype(jnp.bfloat16)
        spec[...] = mul(turned[...].reshape(half * GROUP, 2 * rows), square[...])

    for copy in inputs[2:7]:
        copy.wait()

    def filter_group(g):
        arrived(h_recv.at[g], h_sem.at[g])
        forward(h_recv[g], spec_h.at[g])

    loop(groups, filter_group)
    for g in range(1, groups):
        arrived(d_send.at[g - 1, pl.ds(0, blocks - 1)], send_sem.at[2])
        send_driven(g)

    def driven_group(g):
        arrived(d_recv.at[g], d_sem.at[g])
        forward(d_recv[g], spec_d)
        a, b = spec_d[:, :rows], spec_d[:, rows:]
        u, v = spec_h[g, :, :rows], spec_h[g, :, rows:]
        flat = turned.reshape(half * GROUP, 2 * rows)
        flat[:, :rows] = (a * v + b * u).astype(jnp.bfloat16)
        flat[:, rows:] = (a * u - b * v).astype(jnp.bfloat16)
        spec_d[...] = mul(flat[...], square[...])
        back = spec_d.reshape(half, GROUP, 2 * rows)
        for k in range(half):
            c, s = tw_cos[k], tw_sin[k]
            im, re = back[k, :, :rows], back[k, :, rows:]
            wide[k] = (re * c - im * s).astype(jnp.bfloat16)
            if 0 < k < blocks:
                wide[blocks + k] = (im * c + re * s).astype(jnp.bfloat16)
        for p in range(0, quarters, 2):
            y = mul(last[...], wide[:, :, p * TILE:(p + 2) * TILE].reshape(2 * blocks * GROUP, 2 * TILE))
            for q in (p, p + 1):
                part = y[:, (q - p) * TILE:(q - p + 1) * TILE].astype(jnp.bfloat16)
                y_send[q, g] = part.reshape(blocks, GROUP, TILE)

    def give_back(q, g):
        scatter(
            lambda t: y_send.at[q, g, t], y_recv.at[q, g, me], send_sem.at[3], y_sem.at[q, g]
        )

    for g in range(groups):
        driven_group(g)
        loop(quarters, lambda q: give_back(q, g))
    inputs[7].wait()

    def quarter(q):
        return pl.ds(pl.multiple_of(q * TILE, TILE), TILE)

    def project(q, target, start, width):
        columns = pl.ds(pl.multiple_of(target * chans + start, TILE), width)
        return mul(gated[quarter(q)], w[:, columns])

    apart = chans - SHARED

    def gather(q, g):
        arrived(y_recv.at[q, g], y_sem.at[q, g])

        def gate(t):
            i = g * owners + t
            part = y_recv[q, g, pl.ds(t * per, per)].reshape(TILE, TILE).astype(jnp.float32).T
            value = query[quarter(q), lanes(i)] * (part + direct[quarter(q), lanes(i)])
            gated[quarter(q), lanes(i)] = value.astype(jnp.bfloat16)

        loop(owners, gate)
        here = (quarter(q), slice(g * owners * TILE, (g + 1) * owners * TILE))
        push(gated.at[here], gated_mate.at[here], send_sem.at[7], g_sem.at[q, g], mate)

    def opposite(q):
        gather(q, groups - 1)
        terms = project(q, across, SHARED, apart).astype(jnp.bfloat16)
        s1[0, q] = terms[:TILE // 2]
        s1[1, q] = terms[TILE // 2:]
        push(s1.at[0, q], r1.at[0, q], send_sem.at[4], r1_sem.at[0, q], right)
        push(s1.at[1, q], r1.at[1, q], send_sem.at[4], r1_sem.at[1, q], left)

    def beside(q):
        for g in range(groups):
            here = (quarter(q), slice(g * owners * TILE, (g + 1) * owners * TILE))
            arrived(gated_mate.at[here], g_sem.at[q, g])
        theirs = gated_mate[quarter(q)]
        terms = project(q, pair, 0, SHARED) + mul(theirs, w_mate[1])
        pair_send[quarter(q)] = terms.astype(jnp.bfloat16)
        push(pair_send.at[quarter(q)], pair_recv.at[quarter(q)], send_sem.at[8], p_sem.at[q], pair)
        for side, (target, lo, hi) in enumerate([(right, 0, TILE // 2), (left, TILE // 2, TILE)]):
            terms = project(q, target, SHARED, apart)
            arrived(r1.at[side, q], r1_sem.at[side, q])
            s2[side, q, lo:hi] = (terms[lo:hi] + r1[side, q].astype(jnp.float32)).astype(jnp.bfloat16)
            other = slice(TILE // 2 - lo, TILE + TILE // 2 - hi)
            s2[side, q, other] = terms[other].astype(jnp.bfloat16)
            push(s2.at[side, q], r2.at[side, q], send_sem.at[5], r2_sem.at[side, q], target)
        own[quarter(q), :SHARED] = project(q, x, 0, SHARED) + mul(theirs, w_mate[0])
        own[quarter(q), SHARED:] = project(q, x, SHARED, apart)

    for g in range(groups - 1):
        loop(quarters, lambda q: gather(q, g))
    loop(AHEAD, opposite)
    for i in range(2):
        arrived(w_mate.at[i], w_sem.at[i])

    def steady(q):
        opposite(q + AHEAD)
        beside(q)

    if AHEAD < quarters:
        loop(quarters - AHEAD, steady)
    loop(quarters, beside, quarters - AHEAD)

    def finish(q):
        arrived(pair_recv.at[quarter(q)], p_sem.at[q])
        total = own[quarter(q), :SHARED] + pair_recv[quarter(q)].astype(jnp.float32)
        out_ref[quarter(q), :SHARED] = total.astype(out_ref.dtype)
        for side in range(2):
            arrived(r2.at[side, q], r2_sem.at[side, q])
        total = own[quarter(q), SHARED:] + r2[0, q].astype(jnp.float32) + r2[1, q].astype(jnp.float32)
        out_ref[quarter(q), SHARED:] = total.astype(out_ref.dtype)

    loop(quarters, finish)

    halo_copy.wait_send()
    arrived(d_send.at[groups - 1, pl.ds(0, blocks - 1)], send_sem.at[2])
    arrived(y_send.at[:, :, pl.ds(0, blocks - 1)], send_sem.at[3])
    arrived(s1, send_sem.at[4])
    arrived(s2, send_sem.at[5])
    arrived(w_mate, send_sem.at[6])
    arrived(gated, send_sem.at[7])
    arrived(pair_send, send_sem.at[8])


def on_device(branches, short_kernel, long_filter, skip_gain, out_weight):
    blocks, ring = lax.axis_size("ctx"), lax.axis_size("ch")
    rows, _, chans = branches.shape
    half, quarters, groups = blocks + 1, rows // TILE, chans // blocks // GROUP
    bf16, f32 = jnp.bfloat16, jnp.float32
    consts = tables(blocks, rows)
    anywhere, vmem = pl.BlockSpec(memory_space=pl.ANY), pl.BlockSpec(memory_space=pltpu.VMEM)
    dma = pltpu.SemaphoreType.DMA
    scratch = [
        pltpu.VMEM((3, rows, chans), bf16),
        pltpu.VMEM((rows, chans), f32),
        pltpu.VMEM(out_weight.shape, bf16),
        *[pltpu.VMEM(t.shape, t.dtype) for t in consts],
        pltpu.VMEM((3, GROUP, chans), bf16),
        *[pltpu.VMEM((groups, blocks, GROUP, rows), bf16)] * 4,
        *[pltpu.VMEM((quarters, groups, blocks, GROUP, TILE), bf16)] * 2,
        pltpu.VMEM((rows, chans), f32),
        pltpu.VMEM((rows, chans), f32),
        pltpu.VMEM((rows, chans), bf16),
        pltpu.VMEM((rows, chans), f32),
        pltpu.VMEM((2 * blocks, GROUP, rows), f32),
        pltpu.VMEM((half, GROUP, 2 * rows), bf16),
        pltpu.VMEM((half * GROUP, 2 * rows), f32),
        pltpu.VMEM((groups, half * GROUP, 2 * rows), f32),
        pltpu.VMEM((2 * blocks, GROUP, rows), bf16),
        pltpu.VMEM((2, chans, SHARED), bf16),
        pltpu.VMEM((rows, chans), bf16),
        *[pltpu.VMEM((rows, SHARED), bf16)] * 2,
        *[pltpu.VMEM((2, quarters, TILE // 2, chans - SHARED), bf16)] * 2,
        *[pltpu.VMEM((2, quarters, TILE, chans - SHARED), bf16)] * 2,
        dma((8,)), dma((1,)), dma((groups,)), dma((groups,)), dma((quarters, groups)),
        dma((2,)), dma((quarters, groups)), dma((quarters,)), dma((2, quarters)), dma((2, quarters)), dma((9,)),
    ]
    return pl.pallas_call(
        functools.partial(kernel, blocks, ring),
        out_shape=pltpu.VMEM((rows, chans), bf16),
        in_specs=[anywhere, vmem, anywhere, vmem] + [anywhere] * 6,
        out_specs=vmem,
        scratch_shapes=scratch,
        compiler_params=pltpu.CompilerParams(
            collective_id=0, has_side_effects=True, vmem_limit_bytes=60 * 2**20
        ),
        name="hyena_operator",
    )(
        jnp.transpose(branches, (1, 0, 2)), short_kernel, long_filter, skip_gain.reshape(1, chans),
        out_weight, *consts,
    )


def solution(mesh):
    placed = (P("ctx", None, "ch"), P(None, None, "ch"), P("ctx", "ch"), P("ch"), P("ch", None))
    return jax.shard_map(
        on_device, mesh=mesh, in_specs=placed, out_specs=P("ctx", "ch"), check_vma=False
    )
```

```python
import functools

import jax
import jax.numpy as jnp
import ml_dtypes
import numpy as np
from jax import lax
from jax.experimental import pallas as pl
from jax.experimental.pallas import tpu as pltpu
from jax.sharding import PartitionSpec as P

MESH = pl.DeviceIdType.MESH
GROUP = 16
TILE = 128
STRIDE = 13
SPREAD = 7
INVERSE = 23
AHEAD = 2
SHARED = 768


def tables(blocks, rows):
    classes = 2 * blocks
    half = blocks + 1
    length = classes * rows
    ids, places, blk = np.arange(half), np.arange(rows), np.arange(blocks)
    col = 2.0 * np.pi / classes * (np.outer(ids, blk) % classes)
    eye = np.eye(GROUP)
    first = np.concatenate([np.cos(col), -np.sin(col)[1:blocks]])
    weight = np.full((half, 1), 2.0)
    weight[0] = weight[blocks] = 1.0
    last = np.concatenate([weight * np.cos(col), (-weight * np.sin(col))[1:blocks]]).T / length
    twist = 2.0 * np.pi / length * (np.outer(ids, places) % length)
    inner = 2.0 * np.pi / rows * (np.outer(places, places) % rows)
    cos, sin = np.cos(inner), np.sin(inner)
    square = np.block([[cos, -sin], [sin, cos]])
    return (
        np.kron(first, eye).astype(ml_dtypes.bfloat16),
        np.kron(last, eye).astype(ml_dtypes.bfloat16),
        square.astype(ml_dtypes.bfloat16),
        np.cos(twist).astype(np.float32)[:, None, :],
        np.sin(twist).astype(np.float32)[:, None, :],
    )


def mul(left, right):
    return jnp.dot(left, right, preferred_element_type=jnp.float32)


def loop(count, body, start=0):
    def step(i, carry):
        body(i)
        return carry

    lax.fori_loop(start, count, step, 0)


def kernel(
    blocks, ring,
    br_in, taps_in, filt_in, skip_in, w_in, first_in, last_in, square_in, cos_in, sin_in,
    out_ref,
    br, filt, w, first, last, square, tw_cos, tw_sin, taps_ref, skip_ref,
    halo, h_send, d_send, h_recv, d_recv, y_send, y_recv,
    query, direct, gated, own,
    col, turned, spec_d, spec_h, wide,
    w_mate, gated_mate, pair_send, pair_recv, s1, r1, s2, r2,
    in_sem, halo_sem, h_sem, d_sem, y_sem, w_sem, g_sem, p_sem, r1_sem, r2_sem, send_sem,
):
    me = lax.axis_index("ctx")
    x = lax.axis_index("ch")
    _, rows, chans = br.shape
    groups = chans // blocks // GROUP
    per = TILE // GROUP
    owners = blocks // per
    half = blocks + 1
    quarters = rows // TILE
    right, left, across = lax.rem(x + 1, ring), lax.rem(x + ring - 1, ring), lax.rem(x + ring // 2, ring)
    swap = lax.rem(x, 2) * lax.rem(me + 1, 2) + lax.rem(x + 1, 2) * lax.rem(me, 2)
    mate, pair = right + swap * (left - right), left + swap * (right - left)

    inputs = [
        pltpu.make_async_copy(src, dst, in_sem.at[i])
        for i, (src, dst) in enumerate([
            (filt_in, filt), (taps_in, taps_ref), (skip_in, skip_ref), (br_in, br), (first_in, first), (cos_in, tw_cos), (sin_in, tw_sin),
            (square_in, square), (last_in, last), (w_in, w),
        ])
    ]
    for copy in inputs[:4]:
        copy.start()

    barrier = pltpu.get_barrier_semaphore()

    def greet(k):
        pl.semaphore_signal(
            barrier, inc=1, device_id={"ctx": lax.rem(me + k, blocks)}, device_id_type=MESH
        )

    for side in (left, right):
        pl.semaphore_signal(barrier, inc=1, device_id={"ch": side}, device_id_type=MESH)
    loop(blocks, greet, 1)

    def lanes(i):
        return pl.ds(pl.multiple_of(i * TILE, TILE), TILE)

    def feature(r, i):
        here = slice(r * TILE, (r + 1) * TILE)
        feats = []
        for b in range(3):
            if r:
                part = br[b, r * TILE - GROUP:(r + 1) * TILE, lanes(i)].astype(jnp.float32)
            else:
                before = halo[b, :, lanes(i)].astype(jnp.float32)
                before = jnp.where(me > 0, before, jnp.zeros_like(before))
                part = jnp.concatenate([before, br[b, here, lanes(i)].astype(jnp.float32)], axis=0)
            total = taps_ref[0, b:b + 1, lanes(i)] * part[GROUP:]
            for j in (1, 2):
                total = total + taps_ref[j, b:b + 1, lanes(i)] * pltpu.roll(part, j, 0)[GROUP:]
            feats.append(total)
        driven = feats[1] * feats[2]
        query[here, lanes(i)] = feats[0]
        direct[here, lanes(i)] = skip_ref[:, lanes(i)] * driven
        g, t = i // owners, lax.rem(i, owners) * per
        d_send[g, pl.ds(t, per), :, here] = driven.T.astype(jnp.bfloat16).reshape(per, GROUP, TILE)

    def ctx_copy(src, dst, send, recv, t):
        return pltpu.make_async_remote_copy(
            src_ref=src, dst_ref=dst, send_sem=send, recv_sem=recv,
            device_id={"ctx": t}, device_id_type=MESH,
        )

    def place(t):
        return lax.rem(t * INVERSE, blocks)

    def scatter(src, dst, send, recv):
        def one(k):
            t = lax.rem(me + k * STRIDE, blocks)
            ctx_copy(src(t), dst, send, recv, t).start()

        loop(blocks, one, 1)
        pltpu.make_async_copy(src(me), dst, recv).start()

    def push(src, dst, send, recv, side):
        pltpu.make_async_remote_copy(
            src_ref=src, dst_ref=dst, send_sem=send, recv_sem=recv,
            device_id={"ch": side}, device_id_type=MESH,
        ).start()

    def arrived(ref, sem):
        pltpu.make_async_copy(ref, ref, sem).wait()

    halo_copy = ctx_copy(
        br_in.at[:, pl.ds(rows - GROUP, GROUP), :], halo, send_sem.at[0], halo_sem.at[0],
        lax.rem(me + 1, blocks),
    )

    def turn_filter(k):
        g, t = k // owners, lax.rem(me // per + k, owners)
        i = g * owners + t
        for r in range(quarters):
            here = slice(r * TILE, (r + 1) * TILE)
            turned_part = filt[here, lanes(i)].T.astype(jnp.bfloat16)
            h_send[g, pl.ds(t * per, per), :, here] = turned_part.reshape(per, GROUP, TILE)

        def one(j):
            here = t * per + lax.rem(me + j, per)
            to = lax.rem(here * SPREAD, blocks)
            src, dst = h_send.at[g, here], h_recv.at[g, me]

            @pl.when(to == me)
            def _():
                pltpu.make_async_copy(src, dst, h_sem.at[g]).start()

            @pl.when(to != me)
            def _():
                ctx_copy(src, dst, send_sem.at[1], h_sem.at[g], to).start()

        loop(per, one)

    pl.semaphore_wait(barrier, blocks - 1 + 2)
    for i, target in enumerate((mate, across)):
        push(
            w_in.at[:, pl.ds(pl.multiple_of(target * chans, chans), SHARED)], w_mate.at[i],
            send_sem.at[6], w_sem.at[i], mate,
        )
    halo_copy.start()
    inputs[0].wait()
    loop(chans // TILE, turn_filter)
    for copy in inputs[4:]:
        copy.start()
    for copy in inputs[1:4]:
        copy.wait()
    for r in range(1, quarters):
        loop(chans // TILE, functools.partial(feature, r))
    halo_copy.wait_recv()
    loop(chans // TILE, functools.partial(feature, 0))
    def send_driven(g):
        scatter(lambda t: d_send.at[g, place(t)], d_recv.at[g, me], send_sem.at[2], d_sem.at[g])

    arrived(h_send.at[:, pl.ds(0, blocks - 1)], send_sem.at[1])
    send_driven(0)

    def forward(blocks_in, spec):
        col[...] = mul(first[...], blocks_in.reshape(blocks * GROUP, rows)).reshape(2 * blocks, GROUP, rows)
        for k in range(half):
            c, s = tw_cos[k], tw_sin[k]
            re = col[k]
            if 0 < k < blocks:
                im = col[blocks + k]
                a, b = re * c + im * s, im * c - re * s
            else:
                a, b = re * c, -(re * s)
            turned[k, :, :rows] = a.astype(jnp.bfloat16)
            turned[k, :, rows:] = b.astype(jnp.bfloat16)
        spec[...] = mul(turned[...].reshape(half * GROUP, 2 * rows), square[...])

    for copy in inputs[4:9]:
        copy.wait()

    def filter_group(g):
        arrived(h_recv.at[g], h_sem.at[g])
        forward(h_recv[g], spec_h.at[g])

    loop(groups, filter_group)
    for g in range(1, groups):
        arrived(d_send.at[g - 1, pl.ds(0, blocks - 1)], send_sem.at[2])
        send_driven(g)

    def driven_group(g):
        arrived(d_recv.at[g], d_sem.at[g])
        forward(d_recv[g], spec_d)
        a, b = spec_d[:, :rows], spec_d[:, rows:]
        u, v = spec_h[g, :, :rows], spec_h[g, :, rows:]
        flat = turned.reshape(half * GROUP, 2 * rows)
        flat[:, :rows] = (a * v + b * u).astype(jnp.bfloat16)
        flat[:, rows:] = (a * u - b * v).astype(jnp.bfloat16)
        spec_d[...] = mul(flat[...], square[...])
        back = spec_d.reshape(half, GROUP, 2 * rows)
        for k in range(half):
            c, s = tw_cos[k], tw_sin[k]
            im, re = back[k, :, :rows], back[k, :, rows:]
            wide[k] = (re * c - im * s).astype(jnp.bfloat16)
            if 0 < k < blocks:
                wide[blocks + k] = (im * c + re * s).astype(jnp.bfloat16)
        for p in range(0, quarters, 2):
            y = mul(last[...], wide[:, :, p * TILE:(p + 2) * TILE].reshape(2 * blocks * GROUP, 2 * TILE))
            for q in (p, p + 1):
                part = y[:, (q - p) * TILE:(q - p + 1) * TILE].astype(jnp.bfloat16)
                y_send[q, g] = part.reshape(blocks, GROUP, TILE)

    def give_back(q, g):
        scatter(
            lambda t: y_send.at[q, g, t], y_recv.at[q, g, place(me)], send_sem.at[3], y_sem.at[q, g]
        )

    for g in range(groups):
        driven_group(g)
        loop(quarters, lambda q: give_back(q, g))
    inputs[9].wait()

    def quarter(q):
        return pl.ds(pl.multiple_of(q * TILE, TILE), TILE)

    def project(q, target, start, width):
        columns = pl.ds(pl.multiple_of(target * chans + start, TILE), width)
        return mul(gated[quarter(q)], w[:, columns])

    apart = chans - SHARED

    def gather(q, g):
        arrived(y_recv.at[q, g], y_sem.at[q, g])

        def gate(t):
            i = g * owners + t
            part = y_recv[q, g, pl.ds(t * per, per)].reshape(TILE, TILE).astype(jnp.float32).T
            value = query[quarter(q), lanes(i)] * (part + direct[quarter(q), lanes(i)])
            gated[quarter(q), lanes(i)] = value.astype(jnp.bfloat16)

        loop(owners, gate)
        here = (quarter(q), slice(g * owners * TILE, (g + 1) * owners * TILE))
        push(gated.at[here], gated_mate.at[here], send_sem.at[7], g_sem.at[q, g], mate)

    def opposite(q):
        gather(q, groups - 1)
        terms = project(q, across, SHARED, apart).astype(jnp.bfloat16)
        s1[0, q] = terms[:TILE // 2]
        s1[1, q] = terms[TILE // 2:]
        push(s1.at[0, q], r1.at[0, q], send_sem.at[4], r1_sem.at[0, q], right)
        push(s1.at[1, q], r1.at[1, q], send_sem.at[4], r1_sem.at[1, q], left)

    def beside(q):
        for g in range(groups):
            here = (quarter(q), slice(g * owners * TILE, (g + 1) * owners * TILE))
            arrived(gated_mate.at[here], g_sem.at[q, g])
        theirs = gated_mate[quarter(q)]
        terms = project(q, pair, 0, SHARED) + mul(theirs, w_mate[1])
        pair_send[quarter(q)] = terms.astype(jnp.bfloat16)
        push(pair_send.at[quarter(q)], pair_recv.at[quarter(q)], send_sem.at[8], p_sem.at[q], pair)
        for side, (target, lo, hi) in enumerate([(right, 0, TILE // 2), (left, TILE // 2, TILE)]):
            terms = project(q, target, SHARED, apart)
            arrived(r1.at[side, q], r1_sem.at[side, q])
            s2[side, q, lo:hi] = (terms[lo:hi] + r1[side, q].astype(jnp.float32)).astype(jnp.bfloat16)
            other = slice(TILE // 2 - lo, TILE + TILE // 2 - hi)
            s2[side, q, other] = terms[other].astype(jnp.bfloat16)
            push(s2.at[side, q], r2.at[side, q], send_sem.at[5], r2_sem.at[side, q], target)
        own[quarter(q), :SHARED] = project(q, x, 0, SHARED) + mul(theirs, w_mate[0])
        own[quarter(q), SHARED:] = project(q, x, SHARED, apart)

    for g in range(groups - 1):
        loop(quarters, lambda q: gather(q, g))
    loop(AHEAD, opposite)
    for i in range(2):
        arrived(w_mate.at[i], w_sem.at[i])

    def steady(q):
        opposite(q + AHEAD)
        beside(q)

    if AHEAD < quarters:
        loop(quarters - AHEAD, steady)
    loop(quarters, beside, quarters - AHEAD)

    def finish(q):
        arrived(pair_recv.at[quarter(q)], p_sem.at[q])
        total = own[quarter(q), :SHARED] + pair_recv[quarter(q)].astype(jnp.float32)
        out_ref[quarter(q), :SHARED] = total.astype(out_ref.dtype)
        for side in range(2):
            arrived(r2.at[side, q], r2_sem.at[side, q])
        total = own[quarter(q), SHARED:] + r2[0, q].astype(jnp.float32) + r2[1, q].astype(jnp.float32)
        out_ref[quarter(q), SHARED:] = total.astype(out_ref.dtype)

    loop(quarters, finish)

    halo_copy.wait_send()
    arrived(d_send.at[groups - 1, pl.ds(0, blocks - 1)], send_sem.at[2])
    arrived(y_send.at[:, :, pl.ds(0, blocks - 1)], send_sem.at[3])
    arrived(s1, send_sem.at[4])
    arrived(s2, send_sem.at[5])
    arrived(w_mate, send_sem.at[6])
    arrived(gated, send_sem.at[7])
    arrived(pair_send, send_sem.at[8])


def on_device(branches, short_kernel, long_filter, skip_gain, out_weight):
    blocks, ring = lax.axis_size("ctx"), lax.axis_size("ch")
    rows, _, chans = branches.shape
    half, quarters, groups = blocks + 1, rows // TILE, chans // blocks // GROUP
    bf16, f32 = jnp.bfloat16, jnp.float32
    consts = tables(blocks, rows)
    anywhere, vmem = pl.BlockSpec(memory_space=pl.ANY), pl.BlockSpec(memory_space=pltpu.VMEM)
    dma = pltpu.SemaphoreType.DMA
    scratch = [
        pltpu.VMEM((3, rows, chans), bf16),
        pltpu.VMEM((rows, chans), f32),
        pltpu.VMEM(out_weight.shape, bf16),
        *[pltpu.VMEM(t.shape, t.dtype) for t in consts],
        pltpu.VMEM(short_kernel.shape, f32),
        pltpu.VMEM((1, chans), f32),
        pltpu.VMEM((3, GROUP, chans), bf16),
        *[pltpu.VMEM((groups, blocks, GROUP, rows), bf16)] * 4,
        *[pltpu.VMEM((quarters, groups, blocks, GROUP, TILE), bf16)] * 2,
        pltpu.VMEM((rows, chans), f32),
        pltpu.VMEM((rows, chans), f32),
        pltpu.VMEM((rows, chans), bf16),
        pltpu.VMEM((rows, chans), f32),
        pltpu.VMEM((2 * blocks, GROUP, rows), f32),
        pltpu.VMEM((half, GROUP, 2 * rows), bf16),
        pltpu.VMEM((half * GROUP, 2 * rows), f32),
        pltpu.VMEM((groups, half * GROUP, 2 * rows), f32),
        pltpu.VMEM((2 * blocks, GROUP, rows), bf16),
        pltpu.VMEM((2, chans, SHARED), bf16),
        pltpu.VMEM((rows, chans), bf16),
        *[pltpu.VMEM((rows, SHARED), bf16)] * 2,
        *[pltpu.VMEM((2, quarters, TILE // 2, chans - SHARED), bf16)] * 2,
        *[pltpu.VMEM((2, quarters, TILE, chans - SHARED), bf16)] * 2,
        dma((10,)), dma((1,)), dma((groups,)), dma((groups,)), dma((quarters, groups)),
        dma((2,)), dma((quarters, groups)), dma((quarters,)), dma((2, quarters)), dma((2, quarters)), dma((9,)),
    ]
    return pl.pallas_call(
        functools.partial(kernel, blocks, ring),
        out_shape=pltpu.VMEM((rows, chans), bf16),
        in_specs=[anywhere] * 10,
        out_specs=vmem,
        scratch_shapes=scratch,
        compiler_params=pltpu.CompilerParams(
            collective_id=0, has_side_effects=True, vmem_limit_bytes=60 * 2**20
        ),
        name="hyena_operator",
    )(
        jnp.transpose(branches, (1, 0, 2)), short_kernel, long_filter, skip_gain.reshape(1, chans),
        out_weight, *consts,
    )


def solution(mesh):
    placed = (P("ctx", None, "ch"), P(None, None, "ch"), P("ctx", "ch"), P("ch"), P("ch", None))
    return jax.shard_map(
        on_device, mesh=mesh, in_specs=placed, out_specs=P("ctx", "ch"), check_vma=False
    )
```

```python
import functools

import jax
import jax.numpy as jnp
import ml_dtypes
import numpy as np
from jax import lax
from jax.experimental import pallas as pl
from jax.experimental.pallas import tpu as pltpu
from jax.sharding import PartitionSpec as P

MESH = pl.DeviceIdType.MESH
GROUP = 16
TILE = 128
STRIDE = 13
SPREAD = 7
INVERSE = 23
AHEAD = 2
SHARED = 768


def tables(blocks, rows):
    classes = 2 * blocks
    half = blocks + 1
    length = classes * rows
    ids, places, blk = np.arange(half), np.arange(rows), np.arange(blocks)
    col = 2.0 * np.pi / classes * (np.outer(ids, blk) % classes)
    eye = np.eye(GROUP)
    first = np.concatenate([np.cos(col), -np.sin(col)[1:blocks]])
    weight = np.full((half, 1), 2.0)
    weight[0] = weight[blocks] = 1.0
    last = np.concatenate([weight * np.cos(col), (-weight * np.sin(col))[1:blocks]]).T / length
    twist = 2.0 * np.pi / length * (np.outer(ids, places) % length)
    inner = 2.0 * np.pi / rows * (np.outer(places, places) % rows)
    cos, sin = np.cos(inner), np.sin(inner)
    square = np.block([[cos, -sin], [sin, cos]])
    return (
        np.kron(first, eye).astype(ml_dtypes.bfloat16),
        np.kron(last, eye).astype(ml_dtypes.bfloat16),
        square.astype(ml_dtypes.bfloat16),
        np.cos(twist).astype(np.float32)[:, None, :],
        np.sin(twist).astype(np.float32)[:, None, :],
    )


def mul(left, right):
    return jnp.dot(left, right, preferred_element_type=jnp.float32)


def loop(count, body, start=0):
    def step(i, carry):
        body(i)
        return carry

    lax.fori_loop(start, count, step, 0)


def kernel(
    blocks, ring,
    br_in, taps_in, filt_in, skip_in, w_in, first_in, last_in, square_in, cos_in, sin_in,
    out_ref,
    br, filt, w, first, last, square, tw_cos, tw_sin, taps_ref, skip_ref,
    halo, h_send, d_send, h_recv, d_recv, y_send, y_recv,
    query, direct, gated, own,
    col, turned, spec_d, spec_h, wide,
    w_mate, gated_mate, pair_send, pair_recv, s1, r1, s2, r2,
    in_sem, halo_sem, h_sem, d_sem, y_sem, w_sem, g_sem, p_sem, r1_sem, r2_sem, send_sem,
):
    me = lax.axis_index("ctx")
    x = lax.axis_index("ch")
    _, rows, chans = br.shape
    groups = chans // blocks // GROUP
    per = TILE // GROUP
    owners = blocks // per
    half = blocks + 1
    quarters = rows // TILE
    right, left, across = lax.rem(x + 1, ring), lax.rem(x + ring - 1, ring), lax.rem(x + ring // 2, ring)
    swap = lax.rem(x, 2) * lax.rem(me + 1, 2) + lax.rem(x + 1, 2) * lax.rem(me, 2)
    mate, pair = right + swap * (left - right), left + swap * (right - left)

    inputs = [
        pltpu.make_async_copy(src, dst, in_sem.at[i])
        for i, (src, dst) in enumerate([
            (filt_in, filt), (taps_in, taps_ref), (skip_in, skip_ref), (br_in, br), (first_in, first), (cos_in, tw_cos), (sin_in, tw_sin),
            (square_in, square), (last_in, last), (w_in, w),
        ])
    ]
    for copy in inputs[:4]:
        copy.start()

    barrier = pltpu.get_barrier_semaphore()

    def greet(k):
        pl.semaphore_signal(
            barrier, inc=1, device_id={"ctx": lax.rem(me + k, blocks)}, device_id_type=MESH
        )

    for side in (left, right):
        pl.semaphore_signal(barrier, inc=1, device_id={"ch": side}, device_id_type=MESH)
    loop(blocks, greet, 1)

    def lanes(i):
        return pl.ds(pl.multiple_of(i * TILE, TILE), TILE)

    def feature(r, i):
        here = slice(r * TILE, (r + 1) * TILE)
        feats = []
        for b in range(3):
            if r:
                part = br[b, r * TILE - GROUP:(r + 1) * TILE, lanes(i)].astype(jnp.float32)
            else:
                before = halo[b, :, lanes(i)].astype(jnp.float32)
                before = jnp.where(me > 0, before, jnp.zeros_like(before))
                part = jnp.concatenate([before, br[b, here, lanes(i)].astype(jnp.float32)], axis=0)
            total = taps_ref[0, b:b + 1, lanes(i)] * part[GROUP:]
            for j in (1, 2):
                total = total + taps_ref[j, b:b + 1, lanes(i)] * pltpu.roll(part, j, 0)[GROUP:]
            feats.append(total)
        driven = feats[1] * feats[2]
        query[here, lanes(i)] = feats[0]
        direct[here, lanes(i)] = skip_ref[:, lanes(i)] * driven
        g, t = i // owners, lax.rem(i, owners) * per
        d_send[g, pl.ds(t, per), :, here] = driven.T.astype(jnp.bfloat16).reshape(per, GROUP, TILE)

    def ctx_copy(src, dst, send, recv, t):
        return pltpu.make_async_remote_copy(
            src_ref=src, dst_ref=dst, send_sem=send, recv_sem=recv,
            device_id={"ctx": t}, device_id_type=MESH,
        )

    def place(t):
        return lax.rem(t * INVERSE, blocks)

    def scatter(src, dst, send, recv):
        def one(k):
            t = lax.rem(me + k * STRIDE, blocks)
            ctx_copy(src(t), dst, send, recv, t).start()

        loop(blocks, one, 1)
        pltpu.make_async_copy(src(me), dst, recv).start()

    def push(src, dst, send, recv, side):
        pltpu.make_async_remote_copy(
            src_ref=src, dst_ref=dst, send_sem=send, recv_sem=recv,
            device_id={"ch": side}, device_id_type=MESH,
        ).start()

    def arrived(ref, sem):
        pltpu.make_async_copy(ref, ref, sem).wait()

    halo_copy = ctx_copy(
        br_in.at[:, pl.ds(rows - GROUP, GROUP), :], halo, send_sem.at[0], halo_sem.at[0],
        lax.rem(me + 1, blocks),
    )

    def turn_filter(k):
        g, t = k // owners, lax.rem(me // per + k, owners)
        i = g * owners + t
        for r in range(quarters):
            here = slice(r * TILE, (r + 1) * TILE)
            turned_part = filt[here, lanes(i)].T.astype(jnp.bfloat16)
            h_send[g, pl.ds(t * per, per), :, here] = turned_part.reshape(per, GROUP, TILE)

        def one(j):
            here = t * per + lax.rem(me + j, per)
            to = lax.rem(here * SPREAD, blocks)
            src, dst = h_send.at[g, here], h_recv.at[g, me]

            @pl.when(to == me)
            def _():
                pltpu.make_async_copy(src, dst, h_sem.at[g]).start()

            @pl.when(to != me)
            def _():
                ctx_copy(src, dst, send_sem.at[1], h_sem.at[g], to).start()

        loop(per, one)

    pl.semaphore_wait(barrier, blocks - 1 + 2)
    for i, target in ((1, across), (0, mate)):
        push(
            w_in.at[:, pl.ds(pl.multiple_of(target * chans, chans), SHARED)], w_mate.at[i],
            send_sem.at[6], w_sem.at[i], mate,
        )
    halo_copy.start()
    inputs[0].wait()
    loop(chans // TILE, turn_filter)
    for copy in inputs[4:]:
        copy.start()
    for copy in inputs[1:4]:
        copy.wait()
    for r in range(1, quarters):
        loop(chans // TILE, functools.partial(feature, r))
    halo_copy.wait_recv()
    loop(chans // TILE, functools.partial(feature, 0))
    def send_driven(g):
        scatter(lambda t: d_send.at[g, place(t)], d_recv.at[g, me], send_sem.at[2], d_sem.at[g])

    arrived(h_send.at[:, pl.ds(0, blocks - 1)], send_sem.at[1])
    send_driven(0)

    def forward(blocks_in, spec):
        col[...] = mul(first[...], blocks_in.reshape(blocks * GROUP, rows)).reshape(2 * blocks, GROUP, rows)
        for k in range(half):
            c, s = tw_cos[k], tw_sin[k]
            re = col[k]
            if 0 < k < blocks:
                im = col[blocks + k]
                a, b = re * c + im * s, im * c - re * s
            else:
                a, b = re * c, -(re * s)
            turned[k, :, :rows] = a.astype(jnp.bfloat16)
            turned[k, :, rows:] = b.astype(jnp.bfloat16)
        spec[...] = mul(turned[...].reshape(half * GROUP, 2 * rows), square[...])

    for copy in inputs[4:9]:
        copy.wait()

    def filter_group(g):
        arrived(h_recv.at[g], h_sem.at[g])
        forward(h_recv[g], spec_h.at[g])

    loop(groups, filter_group)
    for g in range(1, groups):
        arrived(d_send.at[g - 1, pl.ds(0, blocks - 1)], send_sem.at[2])
        send_driven(g)

    def driven_group(g):
        arrived(d_recv.at[g], d_sem.at[g])
        forward(d_recv[g], spec_d)
        a, b = spec_d[:, :rows], spec_d[:, rows:]
        u, v = spec_h[g, :, :rows], spec_h[g, :, rows:]
        flat = turned.reshape(half * GROUP, 2 * rows)
        flat[:, :rows] = (a * v + b * u).astype(jnp.bfloat16)
        flat[:, rows:] = (a * u - b * v).astype(jnp.bfloat16)
        spec_d[...] = mul(flat[...], square[...])
        back = spec_d.reshape(half, GROUP, 2 * rows)
        for k in range(half):
            c, s = tw_cos[k], tw_sin[k]
            im, re = back[k, :, :rows], back[k, :, rows:]
            wide[k] = (re * c - im * s).astype(jnp.bfloat16)
            if 0 < k < blocks:
                wide[blocks + k] = (im * c + re * s).astype(jnp.bfloat16)
        for p in range(0, quarters, 2):
            y = mul(last[...], wide[:, :, p * TILE:(p + 2) * TILE].reshape(2 * blocks * GROUP, 2 * TILE))
            for q in (p, p + 1):
                part = y[:, (q - p) * TILE:(q - p + 1) * TILE].astype(jnp.bfloat16)
                y_send[q, g] = part.reshape(blocks, GROUP, TILE)

    def give_back(q, g):
        scatter(
            lambda t: y_send.at[q, g, t], y_recv.at[q, g, place(me)], send_sem.at[3], y_sem.at[q, g]
        )

    for g in range(groups):
        driven_group(g)
        loop(quarters, lambda q: give_back(q, g))
    inputs[9].wait()

    def quarter(q):
        return pl.ds(pl.multiple_of(q * TILE, TILE), TILE)

    def project(q, target, start, width):
        columns = pl.ds(pl.multiple_of(target * chans + start, TILE), width)
        return mul(gated[quarter(q)], w[:, columns])

    apart = chans - SHARED

    def gather(q, g):
        arrived(y_recv.at[q, g], y_sem.at[q, g])

        def gate(t):
            i = g * owners + t
            part = y_recv[q, g, pl.ds(t * per, per)].reshape(TILE, TILE).astype(jnp.float32).T
            value = query[quarter(q), lanes(i)] * (part + direct[quarter(q), lanes(i)])
            gated[quarter(q), lanes(i)] = value.astype(jnp.bfloat16)

        loop(owners, gate)
        here = (quarter(q), slice(g * owners * TILE, (g + 1) * owners * TILE))
        push(gated.at[here], gated_mate.at[here], send_sem.at[7], g_sem.at[q, g], mate)

    def opposite(q):
        gather(q, groups - 1)
        terms = project(q, across, SHARED, apart).astype(jnp.bfloat16)
        s1[0, q] = terms[:TILE // 2]
        s1[1, q] = terms[TILE // 2:]
        push(s1.at[0, q], r1.at[0, q], send_sem.at[4], r1_sem.at[0, q], right)
        push(s1.at[1, q], r1.at[1, q], send_sem.at[4], r1_sem.at[1, q], left)

    def beside(q):
        for g in range(groups):
            here = (quarter(q), slice(g * owners * TILE, (g + 1) * owners * TILE))
            arrived(gated_mate.at[here], g_sem.at[q, g])
        theirs = gated_mate[quarter(q)]
        terms = project(q, pair, 0, SHARED) + mul(theirs, w_mate[1])
        pair_send[quarter(q)] = terms.astype(jnp.bfloat16)
        push(pair_send.at[quarter(q)], pair_recv.at[quarter(q)], send_sem.at[8], p_sem.at[q], pair)
        for side, (target, lo, hi) in enumerate([(right, 0, TILE // 2), (left, TILE // 2, TILE)]):
            terms = project(q, target, SHARED, apart)
            arrived(r1.at[side, q], r1_sem.at[side, q])
            s2[side, q, lo:hi] = (terms[lo:hi] + r1[side, q].astype(jnp.float32)).astype(jnp.bfloat16)
            other = slice(TILE // 2 - lo, TILE + TILE // 2 - hi)
            s2[side, q, other] = terms[other].astype(jnp.bfloat16)
            push(s2.at[side, q], r2.at[side, q], send_sem.at[5], r2_sem.at[side, q], target)

        @pl.when(q == 0)
        def _():
            arrived(w_mate.at[0], w_sem.at[0])

        own[quarter(q), :SHARED] = project(q, x, 0, SHARED) + mul(theirs, w_mate[0])
        own[quarter(q), SHARED:] = project(q, x, SHARED, apart)

    for g in range(groups - 1):
        loop(quarters, lambda q: gather(q, g))
    loop(AHEAD, opposite)
    arrived(w_mate.at[1], w_sem.at[1])

    def steady(q):
        opposite(q + AHEAD)
        beside(q)

    if AHEAD < quarters:
        loop(quarters - AHEAD, steady)
    loop(quarters, beside, quarters - AHEAD)

    def finish(q):
        arrived(pair_recv.at[quarter(q)], p_sem.at[q])
        total = own[quarter(q), :SHARED] + pair_recv[quarter(q)].astype(jnp.float32)
        out_ref[quarter(q), :SHARED] = total.astype(out_ref.dtype)
        for side in range(2):
            arrived(r2.at[side, q], r2_sem.at[side, q])
        total = own[quarter(q), SHARED:] + r2[0, q].astype(jnp.float32) + r2[1, q].astype(jnp.float32)
        out_ref[quarter(q), SHARED:] = total.astype(out_ref.dtype)

    loop(quarters, finish)

    halo_copy.wait_send()
    arrived(d_send.at[groups - 1, pl.ds(0, blocks - 1)], send_sem.at[2])
    arrived(y_send.at[:, :, pl.ds(0, blocks - 1)], send_sem.at[3])
    arrived(s1, send_sem.at[4])
    arrived(s2, send_sem.at[5])
    arrived(w_mate, send_sem.at[6])
    arrived(gated, send_sem.at[7])
    arrived(pair_send, send_sem.at[8])


def on_device(branches, short_kernel, long_filter, skip_gain, out_weight):
    blocks, ring = lax.axis_size("ctx"), lax.axis_size("ch")
    rows, _, chans = branches.shape
    half, quarters, groups = blocks + 1, rows // TILE, chans // blocks // GROUP
    bf16, f32 = jnp.bfloat16, jnp.float32
    consts = tables(blocks, rows)
    anywhere, vmem = pl.BlockSpec(memory_space=pl.ANY), pl.BlockSpec(memory_space=pltpu.VMEM)
    dma = pltpu.SemaphoreType.DMA
    scratch = [
        pltpu.VMEM((3, rows, chans), bf16),
        pltpu.VMEM((rows, chans), f32),
        pltpu.VMEM(out_weight.shape, bf16),
        *[pltpu.VMEM(t.shape, t.dtype) for t in consts],
        pltpu.VMEM(short_kernel.shape, f32),
        pltpu.VMEM((1, chans), f32),
        pltpu.VMEM((3, GROUP, chans), bf16),
        *[pltpu.VMEM((groups, blocks, GROUP, rows), bf16)] * 4,
        *[pltpu.VMEM((quarters, groups, blocks, GROUP, TILE), bf16)] * 2,
        pltpu.VMEM((rows, chans), f32),
        pltpu.VMEM((rows, chans), f32),
        pltpu.VMEM((rows, chans), bf16),
        pltpu.VMEM((rows, chans), f32),
        pltpu.VMEM((2 * blocks, GROUP, rows), f32),
        pltpu.VMEM((half, GROUP, 2 * rows), bf16),
        pltpu.VMEM((half * GROUP, 2 * rows), f32),
        pltpu.VMEM((groups, half * GROUP, 2 * rows), f32),
        pltpu.VMEM((2 * blocks, GROUP, rows), bf16),
        pltpu.VMEM((2, chans, SHARED), bf16),
        pltpu.VMEM((rows, chans), bf16),
        *[pltpu.VMEM((rows, SHARED), bf16)] * 2,
        *[pltpu.VMEM((2, quarters, TILE // 2, chans - SHARED), bf16)] * 2,
        *[pltpu.VMEM((2, quarters, TILE, chans - SHARED), bf16)] * 2,
        dma((10,)), dma((1,)), dma((groups,)), dma((groups,)), dma((quarters, groups)),
        dma((2,)), dma((quarters, groups)), dma((quarters,)), dma((2, quarters)), dma((2, quarters)), dma((9,)),
    ]
    return pl.pallas_call(
        functools.partial(kernel, blocks, ring),
        out_shape=pltpu.VMEM((rows, chans), bf16),
        in_specs=[anywhere] * 10,
        out_specs=vmem,
        scratch_shapes=scratch,
        compiler_params=pltpu.CompilerParams(
            collective_id=0, has_side_effects=True, vmem_limit_bytes=60 * 2**20
        ),
        name="hyena_operator",
    )(
        jnp.transpose(branches, (1, 0, 2)), short_kernel, long_filter, skip_gain.reshape(1, chans),
        out_weight, *consts,
    )


def solution(mesh):
    placed = (P("ctx", None, "ch"), P(None, None, "ch"), P("ctx", "ch"), P("ch"), P("ch", None))
    return jax.shard_map(
        on_device, mesh=mesh, in_specs=placed, out_specs=P("ctx", "ch"), check_vma=False
    )
```
